32 devices in a mesh: grp: 2 (over x), ep: 16 (over z, y, core).
Axes of the slice: x: 2, y: 2, z: 4, core: 2. Of those that a mesh axis runs over, the one named last changes fastest.
Arguments:
- states: bfloat16 [2, 1280, 2048], P(None, ('grp', 'ep')), may hold values from -6 to 6
- route_ids: int32 [2, 1280, 8], P(None, ('grp', 'ep')), may hold values from 0 to 15, all different within a row; in each aligned block of 40 rows (0 to 39, 40 to 79, ..., all dimensions but the last counted through in order) at most 30 rows name the same one
- route_gates: float32 [2, 1280, 8], P(None, ('grp', 'ep')), may hold values from 0.02 to 0.3
- moe_gain: float32 [2048], replicated, may hold values from 0.25 to 1.75
- final_gain: float32 [2048], replicated, may hold values from 0.25 to 1.75
- gate_proj: bfloat16 [16, 2048, 512], P('ep', 'grp'), may hold values from -0.125 to 0.125
- up_proj: bfloat16 [16, 2048, 512], P('ep', 'grp'), may hold values from -0.125 to 0.125
- down_proj: bfloat16 [16, 512, 2048], P('ep', 'grp'), may hold values from -0.25 to 0.25
- old_slots: int32 [16], replicated, may hold values from 0 to 15, each once
- new_slots: int32 [16], replicated, may hold values from 0 to 15, each once
- req_lengths: int32 [2, 2, 4], P(None, 'grp'), may hold values from 1 to 320, 640 in all within a row
- head_proj: bfloat16 [2048, 49152], P(None, ('grp', 'ep')), may hold values from -14 to 14
Outputs:
- mixed: bfloat16 [2, 1280, 2048], P(None, ('grp', 'ep'))
- moved_gate: bfloat16 [16, 2048, 512], P('ep', 'grp')
- moved_up: bfloat16 [16, 2048, 512], P('ep', 'grp')
- moved_down: bfloat16 [16, 512, 2048], P('ep', 'grp')
- log_probs: float32 [2, 8, 49152], P(None, None, ('grp', 'ep'))
The draws below stay inside these ranges and needn't reach their ends.
Inputs may be any that keep to these rules, and one draw needn't show every extreme that they name: `route_ids`: in each aligned block of 40 rows (the rows of one device in one batch) no expert is named by more than 30 rows, a bound that some block reaches; the 8 ids of a row differ. `old_slots`: each expert once. `new_slots`: each expert once. `req_lengths`: the 4 lengths of a group in a batch sum to 640, and the largest is 320.
All inputs are finite; a program needn't handle non-finite values.
Results may differ from the reference program's by a relative error of at most 0.0035.
Values may be sent and summed in bfloat16 or wider, within the bound.
A program may use at most 128 MiB of HBM per device.

```python
import math
import jax
import jax.numpy as jnp
import numpy as np
from jax import lax

D = 2048
TOP = 8
FF = 512
VOCAB = 49152
TB = 40
REQS = 4
EXPERTS = 16
TOKENS = 1280
GROUP_TOK = 640
LONGEST = 320
CAP = 30
N_GRP = 2
N_EP = 16


def draw_head_proj(key, part):
    first_key, second_key = jax.random.split(jax.random.fold_in(key, 17))
    base = jnp.clip(jax.random.normal(first_key, (D, VOCAB), jnp.float32), -4.0, 4.0)
    factor = jnp.exp(jax.random.uniform(second_key, (1, VOCAB), jnp.float32, 0.0, math.log(10.0)))
    return (base * factor / math.sqrt(D)).astype(jnp.bfloat16)


def block_levels(own_key, extent, cuts, least, top_value):
    def one(dim, shards_of):
        draws = jax.random.uniform(jax.random.fold_in(jax.random.fold_in(own_key, 6), dim), (shards_of,), jnp.float32, least / len(cuts), top_value / len(cuts))
        return jnp.repeat(jnp.exp(draws), extent[dim] // shards_of).reshape((-1,) + (1,) * (len(extent) - dim - 1))

    level = one(*cuts[0])
    for cut in cuts[1:]:
        level = level * one(*cut)
    return level


def split_up(amount, total, limit, skew):
    loads = [(1 << 20) // math.isqrt(rank ** skew) + 1 for rank in range(2, amount + 1)]
    rest, given = total - limit - (amount - 1), [1] * (amount - 1)
    while rest > 0:
        movable = [i for i in range(amount - 1) if given[i] < limit]
        pool, remaining = sum([loads[i] for i in movable]), rest
        for i in movable:
            addition = min(limit - given[i], max(1, remaining * loads[i] // pool), rest)
            given[i] = given[i] + addition
            rest = rest - addition
    return np.array([limit] + given)


def ragged(rng, number_of, total, bound, slope):
    if number_of == 2:
        one = jax.random.randint(rng, (), max(1, total - bound), min(bound, total - 1) + 1)
        return jnp.stack([one, total - one])
    tallies = jnp.asarray(split_up(number_of, total, bound, slope), jnp.int32)
    couples = (number_of - 1) // 2
    giver, sink = tallies[1:1 + 2 * couples:2], tallies[2:2 + 2 * couples:2]
    room = jnp.minimum(giver - 1, bound - sink)
    shifted = jax.random.randint(jax.random.fold_in(rng, 1), (couples,), 0, 1 << 20) % (room + 1)
    tallies = tallies.at[1:1 + 2 * couples:2].set(giver - shifted).at[2:2 + 2 * couples:2].set(sink + shifted)
    return tallies[jax.random.permutation(jax.random.fold_in(rng, 2), number_of)]


def assign_block(key, own, number, rows, amount, top, reach, slope):
    sequence = jax.random.permutation(key, amount)
    heavy_load, common = portions_of(amount, rows * top, reach, slope, True), portions_of(amount, rows * top, reach, slope, False)
    places = jnp.arange(amount)

    def named(lengths, turn):
        used = int((lengths > 0).sum())
        fixed = max(1, used // 4)
        shifted = fixed + (places - fixed + turn * (used - fixed)) % max(1, amount - fixed)
        return jnp.zeros((amount,), jnp.int32).at[sequence[jnp.where(places < fixed, places, shifted)]].set(jnp.asarray(lengths, jnp.int32))

    lengths = jnp.where(number % 4 == 0, named(heavy_load, number // 4), named(common, number - number // 4 - 1))
    mixed = jax.random.permutation(jax.random.fold_in(own, 3), amount)
    source_of, sink = mixed[0:amount // 2 * 2:2], mixed[1:amount // 2 * 2:2]
    margin = jnp.minimum(lengths[source_of] - 1, reach - lengths[sink]) // 2
    margin = jnp.where((source_of == sequence[0]) | (sink == sequence[0]) | (lengths[sink] == 0), 0, jnp.maximum(margin, 0))
    shifted = jax.random.randint(jax.random.fold_in(own, 4), (amount // 2,), 0, 1 << 20) % (margin + 1)
    lengths = lengths.at[source_of].add(-shifted).at[sink].add(shifted)
    members = jnp.searchsorted(jnp.cumsum(lengths), jnp.arange(rows * top), side="right").astype(jnp.int32)
    table = members.reshape(top, rows).T
    table = table[jax.random.permutation(jax.random.fold_in(own, 1), rows)]
    turn = jax.random.randint(jax.random.fold_in(own, 2), (rows, 1), 0, top)
    return jnp.take_along_axis(table, (jnp.arange(top)[None, :] + turn) % top, axis=1)


def portions_of(number_of, total, reach, lean, full):
    loads = [(1 << 20) // math.isqrt(grade ** lean) + 1 for grade in range(1, number_of + 1)]
    largest = reach if full else min(reach, max(-(-total // number_of), total * loads[0] // sum(loads)))
    least = 1 if total - largest >= number_of - 1 else 0
    given, rest = [largest] + [least] * (number_of - 1), total - largest - least * (number_of - 1)
    while rest > 0:
        candidates = [i for i in range(1, number_of) if given[i] < largest] or [i for i in range(1, number_of) if given[i] < reach]
        mass, left = sum([loads[i] for i in candidates]), rest
        for i in candidates:
            addition = min(reach - given[i], max(1, left * loads[i] // mass), rest)
            given[i] = given[i] + addition
            rest = rest - addition
    return np.array(given)


def noise(own_key, dims, width, bound, cuts=(), held_as=jnp.bfloat16):
    loudness = block_levels(own_key, dims, cuts, -0.22, 0.18) if cuts else 1.0
    result = jax.random.normal(own_key, dims, jnp.float32) * width * loudness
    return jnp.minimum(jnp.maximum(result, -bound), bound).astype(held_as)


def setup_inputs(seed: int = 0) -> dict:
    splits = jax.random.split(jax.random.key(seed), 13)
    states = noise(splits[0], (2, TOKENS, D), 1.0, 6.0, ((1, 32),))
    route_ids_keys = jax.random.split(jax.random.fold_in(splits[1], 1), 2 * TOKENS // TB)
    route_ids_turns = jax.random.permutation(jax.random.fold_in(splits[1], 3), 2 * TOKENS // TB)
    route_ids = jax.vmap(lambda own, number: assign_block(jax.random.fold_in(splits[1], 2), own, number, TB, EXPERTS, TOP, CAP, 2))(route_ids_keys, route_ids_turns).reshape((2, TOKENS, TOP))
    route_gates = jnp.clip(0.02 + 0.28 * jax.random.uniform(splits[2], (2, TOKENS, TOP), jnp.float32) ** block_levels(splits[2], (2, TOKENS, TOP), ((1, 32),), -0.2, 0.2), 0.02, 0.3)
    moe_gain = jnp.clip(1.0 + 0.15 * jax.random.normal(splits[3], (D,), jnp.float32), 0.25, 1.75)
    final_gain = jnp.clip(1.0 + 0.15 * jax.random.normal(splits[4], (D,), jnp.float32), 0.25, 1.75)
    gate_proj = noise(splits[5], (EXPERTS, D, FF), D ** -0.5, 0.125, ((0, 16), (1, 2)))
    up_proj = noise(splits[6], (EXPERTS, D, FF), D ** -0.5, 0.125, ((0, 16), (1, 2)))
    down_proj = noise(splits[7], (EXPERTS, FF, D), FF ** -0.5, 0.25, ((0, 16), (1, 2)))
    old_slots = jax.random.permutation(splits[8], EXPERTS).astype(jnp.int32)
    new_slots = jax.random.permutation(splits[9], EXPERTS).astype(jnp.int32)
    req_lengths = jax.vmap(lambda own: ragged(own, REQS, GROUP_TOK, LONGEST, 2))(jax.random.split(splits[10], 2 * N_GRP)).reshape((2, N_GRP, REQS)).astype(jnp.int32)
    head_proj = draw_head_proj(jax.random.fold_in(splits[12], 71), 0)
    return dict(states=states, route_ids=route_ids, route_gates=route_gates, moe_gain=moe_gain, final_gain=final_gain, gate_proj=gate_proj, up_proj=up_proj, down_proj=down_proj, old_slots=old_slots, new_slots=new_slots, req_lengths=req_lengths, head_proj=head_proj)


def normalize(rows, gain):
    scale = lax.rsqrt(lax.optimization_barrier(jnp.mean(rows * rows, axis=-1, keepdims=True)) + 1e-06)
    return (rows * scale * gain).astype(jnp.bfloat16)

def owner_table(placement):
    ident = jnp.arange(placement.shape[0], dtype=jnp.int32)
    hits = placement[None, :].astype(jnp.int32) == ident[:, None]
    return lax.optimization_barrier(jnp.sum(jnp.where(hits, ident[None, :], 0), axis=1)).astype(jnp.int32)

def reference(states, route_ids, route_gates, moe_gain, final_gain, gate_proj, up_proj, down_proj, old_slots, new_slots, req_lengths, head_proj):
    old_owner = owner_table(old_slots)
    source = old_owner[new_slots.astype(jnp.int32)].astype(jnp.int32)
    moved_gate = gate_proj[source]
    moved_up = up_proj[source]
    moved_down = down_proj[source]
    residual = states.astype(jnp.float32)
    normed = normalize(residual, moe_gain)
    tokens_all = states.shape[1]
    top_count = route_ids.shape[2]
    experts_all = old_slots.shape[0]
    most_rows = CAP * N_GRP * N_EP
    results = []
    for batch_index in range(2):
        flat_ids = route_ids[batch_index].reshape(-1).astype(jnp.int32)
        order = jnp.argsort(flat_ids, stable=True).astype(jnp.int32)
        ident = jnp.arange(experts_all, dtype=jnp.int32)
        counts = lax.optimization_barrier(jnp.sum((flat_ids[None, :] == ident[:, None]).astype(jnp.int32), axis=1)).astype(jnp.int32)
        starts = (jnp.cumsum(counts) - counts).astype(jnp.int32)
        padded = jnp.concatenate([order, jnp.zeros((most_rows,), jnp.int32)])
        flat_gates = route_gates[batch_index].reshape(-1)
        batch_rows = normed[batch_index]

        def one_expert(running, expert):
            picks = lax.dynamic_slice_in_dim(padded, starts[expert], most_rows).astype(jnp.int32)
            valid = jnp.arange(most_rows, dtype=jnp.int32) < counts[expert]
            token_index = (picks // top_count).astype(jnp.int32)
            rows = batch_rows[token_index]
            slot = old_owner[expert]
            gate_vals = jnp.dot(rows, gate_proj[slot], preferred_element_type=jnp.float32)
            up_vals = jnp.dot(rows, up_proj[slot], preferred_element_type=jnp.float32)
            hidden = (jax.nn.silu(gate_vals) * up_vals).astype(jnp.bfloat16)
            expert_out = jnp.dot(hidden, down_proj[slot], preferred_element_type=jnp.float32).astype(jnp.bfloat16)
            expert_out = lax.optimization_barrier(expert_out).astype(jnp.float32)
            weights = jnp.where(valid, flat_gates[picks], 0.0).astype(jnp.float32)
            running = running.at[token_index].add(weights[:, None] * expert_out)
            return (running, None)
        summed, _ = lax.scan(one_expert, jnp.zeros((tokens_all, D), jnp.float32), jnp.arange(experts_all, dtype=jnp.int32))
        results.append((residual[batch_index] + summed).astype(jnp.bfloat16))
    mixed = jnp.stack(results)
    request_ends = jnp.cumsum(req_lengths.astype(jnp.int32), axis=-1) - 1
    request_ends = request_ends + (jnp.arange(N_GRP, dtype=jnp.int32) * GROUP_TOK)[None, :, None]
    request_ends = request_ends.reshape(2, -1).astype(jnp.int32)
    tails = jnp.take_along_axis(mixed, request_ends[:, :, None], axis=1)
    finals = normalize(tails.astype(jnp.float32), final_gain)
    logits = jnp.dot(finals.reshape(-1, D), head_proj, preferred_element_type=jnp.float32)
    top_val = lax.optimization_barrier(jnp.max(logits, axis=1, keepdims=True))
    totals = lax.optimization_barrier(jnp.sum(jnp.exp(logits - top_val), axis=1, keepdims=True))
    log_probs = (logits - top_val - jnp.log(totals)).reshape(2, -1, logits.shape[1])
    return (mixed, moved_gate, moved_up, moved_down, log_probs)
```

```python
import jax
import jax.numpy as jnp
from jax import lax
from jax.sharding import PartitionSpec as P


def normalize(rows, gain):
    scale = lax.rsqrt(jnp.mean(rows * rows, axis=-1, keepdims=True) + 1e-06)
    return (rows * scale * gain).astype(jnp.bfloat16)


def owner_table(placement):
    ident = jnp.arange(placement.shape[0], dtype=jnp.int32)
    hits = placement[None, :] == ident[:, None]
    return jnp.sum(jnp.where(hits, ident[None, :], 0), axis=1)


def exchange(value, axis, bit):
    n = lax.axis_size(axis)
    return lax.ppermute(value, axis, [(i, i ^ bit) for i in range(n)])


def relocate(weights, source):
    n = source.shape[0]
    rows = weights.reshape(n, weights.shape[1] // n, weights.shape[2])
    spread = lax.all_to_all(rows, "ep", split_axis=0, concat_axis=0, tiled=True)
    ordered = jnp.take(spread, source, axis=0)
    moved = lax.all_to_all(ordered, "ep", split_axis=0, concat_axis=0, tiled=True)
    return moved.reshape(weights.shape)


def split_bf16(value):
    high = lax.reduce_precision(value, 8, 7)
    middle = lax.reduce_precision(value - high, 8, 7)
    low = value - high - middle
    return [part.astype(jnp.bfloat16) for part in (high, middle, low)]


def scatter_sum(terms):
    n = lax.axis_size("ep")
    me = lax.axis_index("ep")
    bit = 1
    held = terms
    while bit < n:
        pairs = held.reshape(held.shape[0] // 2, 2, *held.shape[1:])
        mine = (me // bit) % 2
        sent = lax.dynamic_index_in_dim(pairs, 1 - mine, 1, keepdims=False)
        kept = lax.dynamic_index_in_dim(pairs, mine, 1, keepdims=False)
        held = kept + exchange(sent.astype(jnp.bfloat16), "ep", bit).astype(jnp.float32)
        bit *= 2
    return held[0]


def butterfly(value, axis, join):
    bit = 1
    while bit < lax.axis_size(axis):
        value = join(value, exchange(value, axis, bit))
        bit *= 2
    return value


def join_stats(ours, theirs):
    top = jnp.maximum(ours[0], theirs[0])
    total = ours[1] * jnp.exp(ours[0] - top) + theirs[1] * jnp.exp(theirs[0] - top)
    return jnp.stack([top, total])


def per_device(
    states,
    route_ids,
    route_gates,
    moe_gain,
    final_gain,
    gate_proj,
    up_proj,
    down_proj,
    old_slots,
    new_slots,
    req_lengths,
    head_proj,
):
    n_ep = lax.axis_size("ep")
    n_grp = lax.axis_size("grp")
    column = lax.axis_index("ep")
    group = lax.axis_index("grp")
    batches, tok_rows, width = states.shape
    n_slots = old_slots.shape[0]
    old_owner = owner_table(old_slots)
    source = jnp.take(old_owner, new_slots)

    residual = states.astype(jnp.float32)
    normed = normalize(residual, moe_gain).reshape(-1, width)
    chosen = route_ids[..., None] == old_slots
    slot_gates = jnp.sum(jnp.where(chosen, route_gates[..., None], 0.0), axis=2)
    parts = split_bf16(slot_gates.reshape(-1, n_slots))
    extra = -(-len(parts) * n_slots // 128) * 128
    coded = jnp.pad(jnp.concatenate(parts, axis=1), ((0, 0), (0, extra - len(parts) * n_slots)))
    rows = lax.all_gather(
        jnp.concatenate([normed, coded], axis=1), "ep", axis=0, tiled=True
    )
    gate_full = lax.all_gather(gate_proj[0], "grp", axis=0, tiled=True)
    up_full = lax.all_gather(up_proj[0], "grp", axis=0, tiled=True)
    down_full = lax.all_gather(down_proj[0], "grp", axis=0, tiled=True)

    tokens = rows[:, :width]
    codes = rows[:, width : width + len(parts) * n_slots].astype(jnp.float32)
    codes = codes.reshape(-1, len(parts), n_slots)
    own = jnp.arange(n_slots, dtype=jnp.int32) == column
    weight = jnp.sum(jnp.where(own, codes, 0.0), axis=(1, 2))
    gate_vals = jnp.dot(tokens, gate_full, preferred_element_type=jnp.float32)
    up_vals = jnp.dot(tokens, up_full, preferred_element_type=jnp.float32)
    hidden = (jax.nn.silu(gate_vals) * up_vals).astype(jnp.bfloat16)
    outputs = jnp.dot(hidden, down_full, preferred_element_type=jnp.float32)
    terms = (outputs * weight[:, None]).reshape(n_ep, -1, width)
    summed = scatter_sum(terms).reshape(states.shape)
    mixed = (residual + summed).astype(jnp.bfloat16)

    moved = tuple(relocate(weights, source) for weights in (gate_proj, up_proj, down_proj))

    request_ends = jnp.cumsum(req_lengths[:, 0, :], axis=-1) - 1
    local_ends = request_ends - column * tok_rows
    picker = (
        local_ends[:, :, None] == jnp.arange(tok_rows, dtype=jnp.int32)[None, None, :]
    ).astype(jnp.bfloat16)
    tails = jnp.einsum(
        "brt,btd->brd", picker, mixed, preferred_element_type=jnp.float32
    ).astype(jnp.bfloat16)
    add = lambda a, b: a + b
    tails = butterfly(tails, "ep", add)
    here = (jnp.arange(n_grp, dtype=jnp.int32) == group)[None, :, None, None]
    spread = jnp.where(here, tails[:, None], jnp.zeros((), jnp.bfloat16))
    spread = butterfly(spread, "grp", add)
    finals = normalize(spread.reshape(-1, width).astype(jnp.float32), final_gain)
    logits = jnp.dot(finals, head_proj, preferred_element_type=jnp.float32)
    top = jnp.max(logits, axis=1)
    total = jnp.sum(jnp.exp(logits - top[:, None]), axis=1)
    stats = jnp.stack([top, total])
    stats = butterfly(stats, "ep", join_stats)
    stats = butterfly(stats, "grp", join_stats)
    log_probs = (logits - stats[0][:, None] - jnp.log(stats[1])[:, None]).reshape(
        batches, -1, logits.shape[1]
    )
    return (mixed, *moved, log_probs)


def solution(mesh):
    placed = (
        P(None, ("grp", "ep"), None),
        P(None, ("grp", "ep"), None),
        P(None, ("grp", "ep"), None),
        P(),
        P(),
        P("ep", "grp", None),
        P("ep", "grp", None),
        P("ep", "grp", None),
        P(),
        P(),
        P(None, "grp", None),
        P(None, ("grp", "ep")),
    )
    return jax.shard_map(
        per_device,
        mesh=mesh,
        in_specs=placed,
        out_specs=(
            P(None, ("grp", "ep"), None),
            P("ep", "grp", None),
            P("ep", "grp", None),
            P("ep", "grp", None),
            P(None, None, ("grp", "ep")),
        ),
        check_vma=False,
    )
```

```python
import jax
import jax.numpy as jnp
from jax import lax
from jax.sharding import PartitionSpec as P


def normalize(rows, gain):
    scale = lax.rsqrt(jnp.mean(rows * rows, axis=-1, keepdims=True) + 1e-06)
    return (rows * scale * gain).astype(jnp.bfloat16)


def owner_table(placement):
    ident = jnp.arange(placement.shape[0], dtype=jnp.int32)
    hits = placement[None, :] == ident[:, None]
    return jnp.sum(jnp.where(hits, ident[None, :], 0), axis=1)


def exchange(value, axis, bit):
    n = lax.axis_size(axis)
    return lax.ppermute(value, axis, [(i, i ^ bit) for i in range(n)])


def spread_rows(weights):
    n = lax.axis_size("ep")
    rows = weights.reshape(n, weights.shape[1] // n, weights.shape[2])
    return lax.all_to_all(rows, "ep", split_axis=0, concat_axis=0, tiled=True)


def relocate(spread, source, shape):
    ordered = jnp.take(spread, source, axis=0)
    moved = lax.all_to_all(ordered, "ep", split_axis=0, concat_axis=0, tiled=True)
    return moved.reshape(shape)


def gather_rows(held, axis):
    bit = 1
    while bit < lax.axis_size(axis):
        theirs = exchange(held, axis, bit)
        upper = (lax.axis_index(axis) // bit) % 2 == 1
        held = jnp.concatenate(
            [jnp.where(upper, theirs, held), jnp.where(upper, held, theirs)], axis=0
        )
        bit *= 2
    return held


def split_bf16(value):
    high = lax.reduce_precision(value, 8, 7)
    middle = lax.reduce_precision(value - high, 8, 7)
    low = value - high - middle
    return [part.astype(jnp.bfloat16) for part in (high, middle, low)]


def scatter_sum(terms):
    n = lax.axis_size("ep")
    me = lax.axis_index("ep")
    bit = 1
    held = terms
    while bit < n:
        pairs = held.reshape(held.shape[0] // 2, 2, *held.shape[1:])
        mine = (me // bit) % 2
        sent = lax.dynamic_index_in_dim(pairs, 1 - mine, 1, keepdims=False)
        kept = lax.dynamic_index_in_dim(pairs, mine, 1, keepdims=False)
        held = kept + exchange(sent.astype(jnp.bfloat16), "ep", bit).astype(jnp.float32)
        bit *= 2
    return held[0]


def butterfly(value, axis, join):
    bit = 1
    while bit < lax.axis_size(axis):
        value = join(value, exchange(value, axis, bit))
        bit *= 2
    return value


def join_stats(ours, theirs):
    top = jnp.maximum(ours[0], theirs[0])
    total = ours[1] * jnp.exp(ours[0] - top) + theirs[1] * jnp.exp(theirs[0] - top)
    return jnp.stack([top, total])


def per_device(
    states,
    route_ids,
    route_gates,
    moe_gain,
    final_gain,
    gate_proj,
    up_proj,
    down_proj,
    old_slots,
    new_slots,
    req_lengths,
    head_proj,
):
    n_ep = lax.axis_size("ep")
    n_grp = lax.axis_size("grp")
    column = lax.axis_index("ep")
    group = lax.axis_index("grp")
    batches, tok_rows, width = states.shape
    n_slots = old_slots.shape[0]
    old_owner = owner_table(old_slots)
    source = jnp.take(old_owner, new_slots)

    residual = states.astype(jnp.float32)
    normed = normalize(residual, moe_gain).reshape(-1, width)
    chosen = route_ids[..., None] == old_slots
    slot_gates = jnp.sum(jnp.where(chosen, route_gates[..., None], 0.0), axis=2)
    parts = split_bf16(slot_gates.reshape(-1, n_slots))
    extra = -(-len(parts) * n_slots // 128) * 128
    coded = jnp.pad(jnp.concatenate(parts, axis=1), ((0, 0), (0, extra - len(parts) * n_slots)))
    rows = lax.all_gather(
        jnp.concatenate([normed, coded], axis=1), "ep", axis=0, tiled=True
    )
    gate_full = gather_rows(gate_proj[0], "grp")
    up_full = gather_rows(up_proj[0], "grp")
    down_full = gather_rows(down_proj[0], "grp")
    spread = tuple(spread_rows(weights) for weights in (gate_proj, up_proj, down_proj))
    rows, spread = lax.optimization_barrier((rows, spread))

    tokens = rows[:, :width]
    codes = rows[:, width : width + len(parts) * n_slots].astype(jnp.float32)
    codes = codes.reshape(-1, len(parts), n_slots)
    own = jnp.arange(n_slots, dtype=jnp.int32) == column
    weight = jnp.sum(jnp.where(own, codes, 0.0), axis=(1, 2))
    gate_vals = jnp.dot(tokens, gate_full, preferred_element_type=jnp.float32)
    up_vals = jnp.dot(tokens, up_full, preferred_element_type=jnp.float32)
    hidden = (jax.nn.silu(gate_vals) * up_vals).astype(jnp.bfloat16)
    outputs = jnp.dot(hidden, down_full, preferred_element_type=jnp.float32)
    terms = (outputs * weight[:, None]).reshape(n_ep, -1, width)
    summed = scatter_sum(terms).reshape(states.shape)
    mixed = (residual + summed).astype(jnp.bfloat16)

    moved = tuple(
        relocate(part, source, weights.shape)
        for part, weights in zip(spread, (gate_proj, up_proj, down_proj))
    )

    request_ends = jnp.cumsum(req_lengths[:, 0, :], axis=-1) - 1
    local_ends = request_ends - column * tok_rows
    picker = (
        local_ends[:, :, None] == jnp.arange(tok_rows, dtype=jnp.int32)[None, None, :]
    ).astype(jnp.bfloat16)
    tails = jnp.einsum(
        "brt,btd->brd", picker, mixed, preferred_element_type=jnp.float32
    ).astype(jnp.bfloat16)
    add = lambda a, b: a + b
    tails = butterfly(tails, "ep", add)
    here = (jnp.arange(n_grp, dtype=jnp.int32) == group)[None, :, None, None]
    placed = jnp.where(here, tails[:, None], jnp.zeros((), jnp.bfloat16))
    placed = butterfly(placed, "grp", add)
    finals = normalize(placed.reshape(-1, width).astype(jnp.float32), final_gain)
    logits = jnp.dot(finals, head_proj, preferred_element_type=jnp.float32)
    top = jnp.max(logits, axis=1)
    total = jnp.sum(jnp.exp(logits - top[:, None]), axis=1)
    stats = jnp.stack([top, total])
    stats = butterfly(stats, "ep", join_stats)
    stats = butterfly(stats, "grp", join_stats)
    log_probs = (logits - stats[0][:, None] - jnp.log(stats[1])[:, None]).reshape(
        batches, -1, logits.shape[1]
    )
    return (mixed, *moved, log_probs)


def solution(mesh):
    placed = (
        P(None, ("grp", "ep"), None),
        P(None, ("grp", "ep"), None),
        P(None, ("grp", "ep"), None),
        P(),
        P(),
        P("ep", "grp", None),
        P("ep", "grp", None),
        P("ep", "grp", None),
        P(),
        P(),
        P(None, "grp", None),
        P(None, ("grp", "ep")),
    )
    return jax.shard_map(
        per_device,
        mesh=mesh,
        in_specs=placed,
        out_specs=(
            P(None, ("grp", "ep"), None),
            P("ep", "grp", None),
            P("ep", "grp", None),
            P("ep", "grp", None),
            P(None, None, ("grp", "ep")),
        ),
        check_vma=False,
    )
```

```python
import functools

import jax
import jax.numpy as jnp
from jax import lax
from jax.experimental import pallas as pl
from jax.experimental.pallas import tpu as pltpu
from jax.sharding import PartitionSpec as P

MESH = pl.DeviceIdType.MESH


def normalize(rows, gain):
    scale = lax.rsqrt(jnp.mean(rows * rows, axis=-1, keepdims=True) + 1e-06)
    return (rows * scale * gain).astype(jnp.bfloat16)


def owner_table(placement):
    ident = jnp.arange(placement.shape[0], dtype=jnp.int32)
    hits = placement[None, :] == ident[:, None]
    return jnp.sum(jnp.where(hits, ident[None, :], 0), axis=1)


def exchange(value, axis, bit):
    n = lax.axis_size(axis)
    return lax.ppermute(value, axis, [(i, i ^ bit) for i in range(n)])


def spread_rows(weights):
    n = lax.axis_size("ep")
    rows = weights.reshape(n, weights.shape[1] // n, weights.shape[2])
    return lax.all_to_all(rows, "ep", split_axis=0, concat_axis=0, tiled=True)


def relocate(spread, source, shape):
    ordered = jnp.take(spread, source, axis=0)
    moved = lax.all_to_all(ordered, "ep", split_axis=0, concat_axis=0, tiled=True)
    return moved.reshape(shape)


def gather_rows(held, axis):
    bit = 1
    while bit < lax.axis_size(axis):
        theirs = exchange(held, axis, bit)
        upper = (lax.axis_index(axis) // bit) % 2 == 1
        held = jnp.concatenate(
            [jnp.where(upper, theirs, held), jnp.where(upper, held, theirs)], axis=0
        )
        bit *= 2
    return held


def split_bf16(value):
    high = lax.reduce_precision(value, 8, 7)
    middle = lax.reduce_precision(value - high, 8, 7)
    low = value - high - middle
    return [part.astype(jnp.bfloat16) for part in (high, middle, low)]


def scatter_sum(terms):
    n = lax.axis_size("ep")
    me = lax.axis_index("ep")
    bit = 1
    held = terms
    while bit < n:
        pairs = held.reshape(held.shape[0] // 2, 2, *held.shape[1:])
        mine = (me // bit) % 2
        sent = lax.dynamic_index_in_dim(pairs, 1 - mine, 1, keepdims=False)
        kept = lax.dynamic_index_in_dim(pairs, mine, 1, keepdims=False)
        held = kept + exchange(sent.astype(jnp.bfloat16), "ep", bit).astype(jnp.float32)
        bit *= 2
    return held[0]


def bits_of(size):
    bits = []
    while 2 ** len(bits) < size:
        bits.append(2 ** len(bits))
    return bits


def tail_kernel(
    ep_bits, grp_bits, tails_ref, gain_ref, head_ref, out_ref, held, came, stat, stat_came,
    send_sem, recv_sem,
):
    grp, ep = lax.axis_index("grp"), lax.axis_index("ep")
    partners = [(grp, ep + bit * (1 - 2 * ((ep // bit) % 2))) for bit in ep_bits]
    partners += [(grp + bit * (1 - 2 * ((grp // bit) % 2)), ep) for bit in grp_bits]
    rounds = len(partners)
    barrier = pltpu.get_barrier_semaphore()
    for partner in partners:
        pl.semaphore_signal(barrier, inc=1, device_id=partner, device_id_type=MESH)
    pl.semaphore_wait(barrier, rounds)

    def swap(source, target, slot, partner):
        copy = pltpu.make_async_remote_copy(
            src_ref=source,
            dst_ref=target,
            send_sem=send_sem.at[slot],
            recv_sem=recv_sem.at[slot],
            device_id=partner,
            device_id_type=MESH,
        )
        copy.start()
        copy.wait()

    held[0] = tails_ref[...]
    for step, partner in enumerate(partners):
        swap(held.at[step], came.at[step], step, partner)
        both = held[step].astype(jnp.float32) + came[step].astype(jnp.float32)
        held[step + 1] = both.astype(jnp.bfloat16)
    rows = held[rounds].astype(jnp.float32)
    scale = lax.rsqrt(jnp.mean(rows * rows, axis=-1, keepdims=True) + 1e-06)
    finals = (rows * scale * gain_ref[...]).astype(jnp.bfloat16)
    out_ref[...] = jnp.dot(finals, head_ref[...], preferred_element_type=jnp.float32)
    logits = out_ref[...]
    top = jnp.max(logits, axis=1, keepdims=True)
    total = jnp.sum(jnp.exp(logits - top), axis=1, keepdims=True)
    lanes = stat.shape[2:]
    stat[0, 0] = jnp.broadcast_to(top, lanes)
    stat[0, 1] = jnp.broadcast_to(total, lanes)
    for step, partner in enumerate(partners):
        swap(stat.at[step], stat_came.at[step], rounds + step, partner)
        ours, theirs = stat[step, 0], stat_came[step, 0]
        top = jnp.maximum(ours, theirs)
        stat[step + 1, 0] = top
        stat[step + 1, 1] = stat[step, 1] * jnp.exp(ours - top) + stat_came[step, 1] * jnp.exp(
            theirs - top
        )
    shift = stat[rounds, 0] + jnp.log(stat[rounds, 1])
    out_ref[...] = out_ref[...] - shift[:, :1]


def tail_probs(tails, gain, head):
    ep_bits, grp_bits = bits_of(lax.axis_size("ep")), bits_of(lax.axis_size("grp"))
    rounds = len(ep_bits) + len(grp_bits)
    count, width = tails.shape
    return pl.pallas_call(
        functools.partial(tail_kernel, ep_bits, grp_bits),
        out_shape=jax.ShapeDtypeStruct((count, head.shape[1]), jnp.float32),
        in_specs=[pl.BlockSpec(memory_space=pltpu.VMEM)] * 3,
        out_specs=pl.BlockSpec(memory_space=pltpu.VMEM),
        scratch_shapes=[
            pltpu.VMEM((rounds + 1, count, width), jnp.bfloat16),
            pltpu.VMEM((rounds, count, width), jnp.bfloat16),
            pltpu.VMEM((rounds + 1, 2, count, 128), jnp.float32),
            pltpu.VMEM((rounds, 2, count, 128), jnp.float32),
            pltpu.SemaphoreType.DMA((2 * rounds,)),
            pltpu.SemaphoreType.DMA((2 * rounds,)),
        ],
        compiler_params=pltpu.CompilerParams(
            collective_id=0, has_side_effects=True, vmem_limit_bytes=40 * 2**20
        ),
    )(tails, gain[None, :], head)


def per_device(
    states,
    route_ids,
    route_gates,
    moe_gain,
    final_gain,
    gate_proj,
    up_proj,
    down_proj,
    old_slots,
    new_slots,
    req_lengths,
    head_proj,
):
    n_ep = lax.axis_size("ep")
    n_grp = lax.axis_size("grp")
    column = lax.axis_index("ep")
    group = lax.axis_index("grp")
    batches, tok_rows, width = states.shape
    n_slots = old_slots.shape[0]
    old_owner = owner_table(old_slots)
    source = jnp.take(old_owner, new_slots)

    residual = states.astype(jnp.float32)
    normed = normalize(residual, moe_gain).reshape(-1, width)
    chosen = route_ids[..., None] == old_slots
    slot_gates = jnp.sum(jnp.where(chosen, route_gates[..., None], 0.0), axis=2)
    parts = split_bf16(slot_gates.reshape(-1, n_slots))
    extra = -(-len(parts) * n_slots // 128) * 128
    coded = jnp.pad(jnp.concatenate(parts, axis=1), ((0, 0), (0, extra - len(parts) * n_slots)))
    rows = lax.all_gather(
        jnp.concatenate([normed, coded], axis=1), "ep", axis=0, tiled=True
    )
    gate_full = gather_rows(gate_proj[0], "grp")
    up_full = gather_rows(up_proj[0], "grp")
    down_full = gather_rows(down_proj[0], "grp")
    up_next, gate_full = lax.optimization_barrier((up_proj, gate_full))
    down_next, up_full = lax.optimization_barrier((down_proj, up_full))
    spread = tuple(spread_rows(weights) for weights in (gate_proj, up_next, down_next))
    rows, spread = lax.optimization_barrier((rows, spread))

    tokens = rows[:, :width]
    codes = rows[:, width : width + len(parts) * n_slots].astype(jnp.float32)
    codes = codes.reshape(-1, len(parts), n_slots)
    own = jnp.arange(n_slots, dtype=jnp.int32) == column
    weight = jnp.sum(jnp.where(own, codes, 0.0), axis=(1, 2))
    gate_vals = jnp.dot(tokens, gate_full, preferred_element_type=jnp.float32)
    up_vals = jnp.dot(tokens, up_full, preferred_element_type=jnp.float32)
    hidden = (jax.nn.silu(gate_vals) * up_vals).astype(jnp.bfloat16)
    outputs = jnp.dot(hidden, down_full, preferred_element_type=jnp.float32)
    terms = (outputs * weight[:, None]).reshape(n_ep, -1, width)
    summed = scatter_sum(terms).reshape(states.shape)
    mixed = (residual + summed).astype(jnp.bfloat16)

    moved = tuple(
        relocate(part, source, weights.shape)
        for part, weights in zip(spread, (gate_proj, up_proj, down_proj))
    )

    request_ends = jnp.cumsum(req_lengths[:, 0, :], axis=-1) - 1
    local_ends = request_ends - column * tok_rows
    picker = (
        local_ends[:, :, None] == jnp.arange(tok_rows, dtype=jnp.int32)[None, None, :]
    ).astype(jnp.bfloat16)
    tails = jnp.einsum(
        "brt,btd->brd", picker, mixed, preferred_element_type=jnp.float32
    ).astype(jnp.bfloat16)
    here = (jnp.arange(n_grp, dtype=jnp.int32) == group)[None, :, None, None]
    placed = jnp.where(here, tails[:, None], jnp.zeros((), jnp.bfloat16))
    log_probs = tail_probs(placed.reshape(-1, width), final_gain, head_proj)
    log_probs = log_probs.reshape(batches, -1, log_probs.shape[1])
    return (mixed, *moved, log_probs)


def solution(mesh):
    placed = (
        P(None, ("grp", "ep"), None),
        P(None, ("grp", "ep"), None),
        P(None, ("grp", "ep"), None),
        P(),
        P(),
        P("ep", "grp", None),
        P("ep", "grp", None),
        P("ep", "grp", None),
        P(),
        P(),
        P(None, "grp", None),
        P(None, ("grp", "ep")),
    )
    return jax.shard_map(
        per_device,
        mesh=mesh,
        in_specs=placed,
        out_specs=(
            P(None, ("grp", "ep"), None),
            P("ep", "grp", None),
            P("ep", "grp", None),
            P("ep", "grp", None),
            P(None, None, ("grp", "ep")),
        ),
        check_vma=False,
    )
```

```python
import functools

import jax
import jax.numpy as jnp
from jax import lax
from jax.experimental import pallas as pl
from jax.experimental.pallas import tpu as pltpu
from jax.sharding import PartitionSpec as P

MESH = pl.DeviceIdType.MESH


def normalize(rows, gain):
    scale = lax.rsqrt(jnp.mean(rows * rows, axis=-1, keepdims=True) + 1e-06)
    return (rows * scale * gain).astype(jnp.bfloat16)


def owner_table(placement):
    ident = jnp.arange(placement.shape[0], dtype=jnp.int32)
    hits = placement[None, :] == ident[:, None]
    return jnp.sum(jnp.where(hits, ident[None, :], 0), axis=1)


def exchange(value, axis, bit):
    n = lax.axis_size(axis)
    return lax.ppermute(value, axis, [(i, i ^ bit) for i in range(n)])


def spread_rows(weights):
    n = lax.axis_size("ep")
    rows = weights.reshape(n, weights.shape[1] // n, weights.shape[2])
    return lax.all_to_all(rows, "ep", split_axis=0, concat_axis=0, tiled=True)


def relocate(spread, source, shape):
    ordered = jnp.take(spread, source, axis=0)
    moved = lax.all_to_all(ordered, "ep", split_axis=0, concat_axis=0, tiled=True)
    return moved.reshape(shape)


def gather_rows(held, axis, dim):
    bit = 1
    while bit < lax.axis_size(axis):
        theirs = exchange(held, axis, bit)
        upper = (lax.axis_index(axis) // bit) % 2 == 1
        held = jnp.concatenate(
            [jnp.where(upper, theirs, held), jnp.where(upper, held, theirs)], axis=dim
        )
        bit *= 2
    return held


def split_bf16(value):
    high = lax.reduce_precision(value, 8, 7)
    middle = lax.reduce_precision(value - high, 8, 7)
    low = value - high - middle
    return [part.astype(jnp.bfloat16) for part in (high, middle, low)]


def scatter_sum(terms):
    n = lax.axis_size("ep")
    me = lax.axis_index("ep")
    bit = 1
    held = terms
    while bit < n:
        pairs = held.reshape(held.shape[0] // 2, 2, *held.shape[1:])
        mine = (me // bit) % 2
        sent = lax.dynamic_index_in_dim(pairs, 1 - mine, 1, keepdims=False)
        kept = lax.dynamic_index_in_dim(pairs, mine, 1, keepdims=False)
        held = kept + exchange(sent.astype(jnp.bfloat16), "ep", bit).astype(jnp.float32)
        bit *= 2
    return held[0]


def bits_of(size):
    bits = []
    while 2 ** len(bits) < size:
        bits.append(2 ** len(bits))
    return bits


def tail_kernel(
    ep_bits, grp_bits, tails_ref, gain_ref, head_ref, out_ref, held, came, stat, stat_came,
    send_sem, recv_sem,
):
    grp, ep = lax.axis_index("grp"), lax.axis_index("ep")
    partners = [(grp, ep + bit * (1 - 2 * ((ep // bit) % 2))) for bit in ep_bits]
    partners += [(grp + bit * (1 - 2 * ((grp // bit) % 2)), ep) for bit in grp_bits]
    rounds = len(partners)
    barrier = pltpu.get_barrier_semaphore()
    for partner in partners:
        pl.semaphore_signal(barrier, inc=1, device_id=partner, device_id_type=MESH)
    pl.semaphore_wait(barrier, rounds)

    def swap(source, target, slot, partner):
        copy = pltpu.make_async_remote_copy(
            src_ref=source,
            dst_ref=target,
            send_sem=send_sem.at[slot],
            recv_sem=recv_sem.at[slot],
            device_id=partner,
            device_id_type=MESH,
        )
        copy.start()
        copy.wait()

    held[0] = tails_ref[...]
    for step, partner in enumerate(partners):
        swap(held.at[step], came.at[step], step, partner)
        both = held[step].astype(jnp.float32) + came[step].astype(jnp.float32)
        held[step + 1] = both.astype(jnp.bfloat16)
    rows = held[rounds].astype(jnp.float32)
    scale = lax.rsqrt(jnp.mean(rows * rows, axis=-1, keepdims=True) + 1e-06)
    finals = (rows * scale * gain_ref[...]).astype(jnp.bfloat16)
    out_ref[...] = jnp.dot(finals, head_ref[...], preferred_element_type=jnp.float32)
    logits = out_ref[...]
    top = jnp.max(logits, axis=1, keepdims=True)
    total = jnp.sum(jnp.exp(logits - top), axis=1, keepdims=True)
    lanes = stat.shape[2:]
    stat[0, 0] = jnp.broadcast_to(top, lanes)
    stat[0, 1] = jnp.broadcast_to(total, lanes)
    for step, partner in enumerate(partners):
        swap(stat.at[step], stat_came.at[step], rounds + step, partner)
        ours, theirs = stat[step, 0], stat_came[step, 0]
        top = jnp.maximum(ours, theirs)
        stat[step + 1, 0] = top
        stat[step + 1, 1] = stat[step, 1] * jnp.exp(ours - top) + stat_came[step, 1] * jnp.exp(
            theirs - top
        )
    shift = stat[rounds, 0] + jnp.log(stat[rounds, 1])
    out_ref[...] = out_ref[...] - shift[:, :1]


def tail_probs(tails, gain, head):
    ep_bits, grp_bits = bits_of(lax.axis_size("ep")), bits_of(lax.axis_size("grp"))
    rounds = len(ep_bits) + len(grp_bits)
    count, width = tails.shape
    return pl.pallas_call(
        functools.partial(tail_kernel, ep_bits, grp_bits),
        out_shape=jax.ShapeDtypeStruct((count, head.shape[1]), jnp.float32),
        in_specs=[pl.BlockSpec(memory_space=pltpu.VMEM)] * 3,
        out_specs=pl.BlockSpec(memory_space=pltpu.VMEM),
        scratch_shapes=[
            pltpu.VMEM((rounds + 1, count, width), jnp.bfloat16),
            pltpu.VMEM((rounds, count, width), jnp.bfloat16),
            pltpu.VMEM((rounds + 1, 2, count, 128), jnp.float32),
            pltpu.VMEM((rounds, 2, count, 128), jnp.float32),
            pltpu.SemaphoreType.DMA((2 * rounds,)),
            pltpu.SemaphoreType.DMA((2 * rounds,)),
        ],
        cost_estimate=pl.CostEstimate(
            flops=2 * count * width * head.shape[1],
            bytes_accessed=16 * head.size,
            transcendentals=count * head.shape[1],
        ),
        compiler_params=pltpu.CompilerParams(
            collective_id=0, has_side_effects=True, vmem_limit_bytes=40 * 2**20
        ),
    )(tails, gain[None, :], head)


def per_device(
    states,
    route_ids,
    route_gates,
    moe_gain,
    final_gain,
    gate_proj,
    up_proj,
    down_proj,
    old_slots,
    new_slots,
    req_lengths,
    head_proj,
):
    n_ep = lax.axis_size("ep")
    n_grp = lax.axis_size("grp")
    column = lax.axis_index("ep")
    group = lax.axis_index("grp")
    batches, tok_rows, width = states.shape
    n_slots = old_slots.shape[0]
    old_owner = owner_table(old_slots)
    source = jnp.take(old_owner, new_slots)

    residual = states.astype(jnp.float32)
    normed = normalize(residual, moe_gain).reshape(-1, width)
    chosen = route_ids[..., None] == old_slots
    slot_gates = jnp.sum(jnp.where(chosen, route_gates[..., None], 0.0), axis=2)
    parts = split_bf16(slot_gates.reshape(-1, n_slots))
    extra = -(-len(parts) * n_slots // 128) * 128
    coded = jnp.pad(jnp.concatenate(parts, axis=1), ((0, 0), (0, extra - len(parts) * n_slots)))
    rows = lax.all_gather(
        jnp.concatenate([normed, coded], axis=1), "ep", axis=0, tiled=True
    )
    both_full = gather_rows(jnp.concatenate([gate_proj, up_proj], axis=0), "grp", 1)
    up_next, both_full = lax.optimization_barrier((up_proj, both_full))
    down_full = gather_rows(down_proj[0], "grp", 0)
    gate_full, up_full = both_full[0], both_full[1]
    spread = (spread_rows(gate_proj), spread_rows(up_next))
    rows, spread = lax.optimization_barrier((rows, spread))

    tokens = rows[:, :width]
    codes = rows[:, width : width + len(parts) * n_slots].astype(jnp.float32)
    codes = codes.reshape(-1, len(parts), n_slots)
    own = jnp.arange(n_slots, dtype=jnp.int32) == column
    weight = jnp.sum(jnp.where(own, codes, 0.0), axis=(1, 2))
    gate_vals = jnp.dot(tokens, gate_full, preferred_element_type=jnp.float32)
    up_vals = jnp.dot(tokens, up_full, preferred_element_type=jnp.float32)
    hidden = (jax.nn.silu(gate_vals) * up_vals).astype(jnp.bfloat16)
    down_next, hidden = lax.optimization_barrier((down_proj, hidden))
    down_spread = spread_rows(down_next)
    outputs = jnp.dot(hidden, down_full, preferred_element_type=jnp.float32)
    terms = (outputs * weight[:, None]).reshape(n_ep, -1, width)
    summed = scatter_sum(terms).reshape(states.shape)
    mixed = (residual + summed).astype(jnp.bfloat16)

    down_spread, mixed = lax.optimization_barrier((down_spread, mixed))
    moved = tuple(
        relocate(part, source, weights.shape)
        for part, weights in zip((*spread, down_spread), (gate_proj, up_proj, down_proj))
    )

    request_ends = jnp.cumsum(req_lengths[:, 0, :], axis=-1) - 1
    local_ends = request_ends - column * tok_rows
    picker = (
        local_ends[:, :, None] == jnp.arange(tok_rows, dtype=jnp.int32)[None, None, :]
    ).astype(jnp.bfloat16)
    tails = jnp.einsum(
        "brt,btd->brd", picker, mixed, preferred_element_type=jnp.float32
    ).astype(jnp.bfloat16)
    here = (jnp.arange(n_grp, dtype=jnp.int32) == group)[None, :, None, None]
    placed = jnp.where(here, tails[:, None], jnp.zeros((), jnp.bfloat16))
    log_probs = tail_probs(placed.reshape(-1, width), final_gain, head_proj)
    log_probs = log_probs.reshape(batches, -1, log_probs.shape[1])
    return (mixed, *moved, log_probs)


def solution(mesh):
    placed = (
        P(None, ("grp", "ep"), None),
        P(None, ("grp", "ep"), None),
        P(None, ("grp", "ep"), None),
        P(),
        P(),
        P("ep", "grp", None),
        P("ep", "grp", None),
        P("ep", "grp", None),
        P(),
        P(),
        P(None, "grp", None),
        P(None, ("grp", "ep")),
    )
    return jax.shard_map(
        per_device,
        mesh=mesh,
        in_specs=placed,
        out_specs=(
            P(None, ("grp", "ep"), None),
            P("ep", "grp", None),
            P("ep", "grp", None),
            P("ep", "grp", None),
            P(None, None, ("grp", "ep")),
        ),
        check_vma=False,
    )
```

```python
import functools

import jax
import jax.numpy as jnp
from jax import lax
from jax.experimental import pallas as pl
from jax.experimental.pallas import tpu as pltpu
from jax.sharding import PartitionSpec as P

MESH = pl.DeviceIdType.MESH


def normalize(rows, gain):
    scale = lax.rsqrt(jnp.mean(rows * rows, axis=-1, keepdims=True) + 1e-06)
    return (rows * scale * gain).astype(jnp.bfloat16)


def owner_table(placement):
    ident = jnp.arange(placement.shape[0], dtype=jnp.int32)
    hits = placement[None, :] == ident[:, None]
    return jnp.sum(jnp.where(hits, ident[None, :], 0), axis=1)


def exchange(value, axis, bit):
    n = lax.axis_size(axis)
    return lax.ppermute(value, axis, [(i, i ^ bit) for i in range(n)])


def spread_rows(weights):
    n = lax.axis_size("ep")
    rows = weights.reshape(n, weights.shape[1] // n, weights.shape[2])
    return lax.all_to_all(rows, "ep", split_axis=0, concat_axis=0, tiled=True)


def relocate(spread, source, shape):
    ordered = jnp.take(spread, source, axis=0)
    moved = lax.all_to_all(ordered, "ep", split_axis=0, concat_axis=0, tiled=True)
    return moved.reshape(shape)


def gather_rows(held, axis, dim):
    bit = 1
    while bit < lax.axis_size(axis):
        theirs = exchange(held, axis, bit)
        upper = (lax.axis_index(axis) // bit) % 2 == 1
        held = jnp.concatenate(
            [jnp.where(upper, theirs, held), jnp.where(upper, held, theirs)], axis=dim
        )
        bit *= 2
    return held


def split_bf16(value):
    high = lax.reduce_precision(value, 8, 7)
    middle = lax.reduce_precision(value - high, 8, 7)
    low = value - high - middle
    return [part.astype(jnp.bfloat16) for part in (high, middle, low)]


def scatter_sum(terms):
    n = lax.axis_size("ep")
    me = lax.axis_index("ep")
    bit = 1
    held = terms
    while bit < n:
        pairs = held.reshape(held.shape[0] // 2, 2, *held.shape[1:])
        mine = (me // bit) % 2
        sent = lax.dynamic_index_in_dim(pairs, 1 - mine, 1, keepdims=False)
        kept = lax.dynamic_index_in_dim(pairs, mine, 1, keepdims=False)
        held = kept + exchange(sent.astype(jnp.bfloat16), "ep", bit).astype(jnp.float32)
        bit *= 2
    return held[0]


def bits_of(size):
    bits = []
    while 2 ** len(bits) < size:
        bits.append(2 ** len(bits))
    return bits


def tail_kernel(
    ep_bits, grp_bits, tails_ref, gain_ref, head_ref, out_ref, held, came, stat, stat_came,
    send_sem, recv_sem,
):
    grp, ep = lax.axis_index("grp"), lax.axis_index("ep")
    partners = [(grp, ep + bit * (1 - 2 * ((ep // bit) % 2))) for bit in ep_bits]
    partners += [(grp + bit * (1 - 2 * ((grp // bit) % 2)), ep) for bit in grp_bits]
    rounds = len(partners)
    barrier = pltpu.get_barrier_semaphore()
    for partner in partners:
        pl.semaphore_signal(barrier, inc=1, device_id=partner, device_id_type=MESH)
    pl.semaphore_wait(barrier, rounds)

    def swap(source, target, slot, partner):
        copy = pltpu.make_async_remote_copy(
            src_ref=source,
            dst_ref=target,
            send_sem=send_sem.at[slot],
            recv_sem=recv_sem.at[slot],
            device_id=partner,
            device_id_type=MESH,
        )
        copy.start()
        copy.wait()

    held[0] = tails_ref[...]
    for step, partner in enumerate(partners):
        swap(held.at[step], came.at[step], step, partner)
        both = held[step].astype(jnp.float32) + came[step].astype(jnp.float32)
        held[step + 1] = both.astype(jnp.bfloat16)
    rows = held[rounds].astype(jnp.float32)
    scale = lax.rsqrt(jnp.mean(rows * rows, axis=-1, keepdims=True) + 1e-06)
    finals = (rows * scale * gain_ref[...]).astype(jnp.bfloat16)
    out_ref[...] = jnp.dot(finals, head_ref[...], preferred_element_type=jnp.float32)
    logits = out_ref[...]
    top = jnp.max(logits, axis=1, keepdims=True)
    total = jnp.sum(jnp.exp(logits - top), axis=1, keepdims=True)
    lanes = stat.shape[2:]
    stat[0, 0] = jnp.broadcast_to(top, lanes)
    stat[0, 1] = jnp.broadcast_to(total, lanes)
    for step, partner in enumerate(partners):
        swap(stat.at[step], stat_came.at[step], rounds + step, partner)
        ours, theirs = stat[step, 0], stat_came[step, 0]
        top = jnp.maximum(ours, theirs)
        stat[step + 1, 0] = top
        stat[step + 1, 1] = stat[step, 1] * jnp.exp(ours - top) + stat_came[step, 1] * jnp.exp(
            theirs - top
        )
    shift = stat[rounds, 0] + jnp.log(stat[rounds, 1])
    out_ref[...] = out_ref[...] - shift[:, :1]


def tail_probs(tails, gain, head):
    ep_bits, grp_bits = bits_of(lax.axis_size("ep")), bits_of(lax.axis_size("grp"))
    rounds = len(ep_bits) + len(grp_bits)
    count, width = tails.shape
    return pl.pallas_call(
        functools.partial(tail_kernel, ep_bits, grp_bits),
        out_shape=jax.ShapeDtypeStruct((count, head.shape[1]), jnp.float32),
        in_specs=[pl.BlockSpec(memory_space=pltpu.VMEM)] * 3,
        out_specs=pl.BlockSpec(memory_space=pltpu.VMEM),
        scratch_shapes=[
            pltpu.VMEM((rounds + 1, count, width), jnp.bfloat16),
            pltpu.VMEM((rounds, count, width), jnp.bfloat16),
            pltpu.VMEM((rounds + 1, 2, count, 128), jnp.float32),
            pltpu.VMEM((rounds, 2, count, 128), jnp.float32),
            pltpu.SemaphoreType.DMA((2 * rounds,)),
            pltpu.SemaphoreType.DMA((2 * rounds,)),
        ],
        cost_estimate=pl.CostEstimate(
            flops=2 * count * width * head.shape[1],
            bytes_accessed=16 * head.size,
            transcendentals=count * head.shape[1],
        ),
        compiler_params=pltpu.CompilerParams(
            collective_id=0, has_side_effects=True, vmem_limit_bytes=40 * 2**20
        ),
    )(tails, gain[None, :], head)


def per_device(
    states,
    route_ids,
    route_gates,
    moe_gain,
    final_gain,
    gate_proj,
    up_proj,
    down_proj,
    old_slots,
    new_slots,
    req_lengths,
    head_proj,
):
    n_ep = lax.axis_size("ep")
    n_grp = lax.axis_size("grp")
    column = lax.axis_index("ep")
    group = lax.axis_index("grp")
    batches, tok_rows, width = states.shape
    n_slots = old_slots.shape[0]
    old_owner = owner_table(old_slots)
    source = jnp.take(old_owner, new_slots)

    residual = states.astype(jnp.float32)
    normed = normalize(residual, moe_gain).reshape(-1, width)
    chosen = route_ids[..., None] == old_slots
    slot_gates = jnp.sum(jnp.where(chosen, route_gates[..., None], 0.0), axis=2)
    parts = split_bf16(slot_gates.reshape(-1, n_slots))
    extra = -(-len(parts) * n_slots // 128) * 128
    coded = jnp.pad(jnp.concatenate(parts, axis=1), ((0, 0), (0, extra - len(parts) * n_slots)))
    rows = lax.all_gather(
        jnp.concatenate([normed, coded], axis=1), "ep", axis=0, tiled=True
    )
    both_full = gather_rows(jnp.concatenate([gate_proj, up_proj], axis=0), "grp", 1)
    up_next, both_full = lax.optimization_barrier((up_proj, both_full))
    down_full = gather_rows(down_proj[0], "grp", 0)
    gate_full, up_full = both_full[0], both_full[1]
    spread = (spread_rows(gate_proj), spread_rows(up_next))
    rows, spread = lax.optimization_barrier((rows, spread))

    tokens = rows[:, :width]
    codes = rows[:, width : width + len(parts) * n_slots].astype(jnp.float32)
    codes = codes.reshape(-1, len(parts), n_slots)
    own = jnp.arange(n_slots, dtype=jnp.int32) == column
    weight = jnp.sum(jnp.where(own, codes, 0.0), axis=(1, 2))
    gate_vals = jnp.dot(tokens, gate_full, preferred_element_type=jnp.float32)
    up_vals = jnp.dot(tokens, up_full, preferred_element_type=jnp.float32)
    hidden = (jax.nn.silu(gate_vals) * up_vals).astype(jnp.bfloat16)
    down_next, hidden = lax.optimization_barrier((down_proj, hidden))
    down_spread = spread_rows(down_next)
    outputs = jnp.dot(hidden, down_full, preferred_element_type=jnp.float32)
    terms = (outputs * weight[:, None]).reshape(n_ep, -1, width)
    summed = scatter_sum(terms).reshape(states.shape)
    mixed = (residual + summed).astype(jnp.bfloat16)

    up_spread, down_spread, mixed = lax.optimization_barrier((spread[1], down_spread, mixed))
    moved = tuple(
        relocate(part, source, weights.shape)
        for part, weights in zip((spread[0], up_spread, down_spread), (gate_proj, up_proj, down_proj))
    )

    request_ends = jnp.cumsum(req_lengths[:, 0, :], axis=-1) - 1
    local_ends = request_ends - column * tok_rows
    picker = (
        local_ends[:, :, None] == jnp.arange(tok_rows, dtype=jnp.int32)[None, None, :]
    ).astype(jnp.bfloat16)
    tails = jnp.einsum(
        "brt,btd->brd", picker, mixed, preferred_element_type=jnp.float32
    ).astype(jnp.bfloat16)
    here = (jnp.arange(n_grp, dtype=jnp.int32) == group)[None, :, None, None]
    placed = jnp.where(here, tails[:, None], jnp.zeros((), jnp.bfloat16))
    log_probs = tail_probs(placed.reshape(-1, width), final_gain, head_proj)
    log_probs = log_probs.reshape(batches, -1, log_probs.shape[1])
    return (mixed, *moved, log_probs)


def solution(mesh):
    placed = (
        P(None, ("grp", "ep"), None),
        P(None, ("grp", "ep"), None),
        P(None, ("grp", "ep"), None),
        P(),
        P(),
        P("ep", "grp", None),
        P("ep", "grp", None),
        P("ep", "grp", None),
        P(),
        P(),
        P(None, "grp", None),
        P(None, ("grp", "ep")),
    )
    return jax.shard_map(
        per_device,
        mesh=mesh,
        in_specs=placed,
        out_specs=(
            P(None, ("grp", "ep"), None),
            P("ep", "grp", None),
            P("ep", "grp", None),
            P("ep", "grp", None),
            P(None, None, ("grp", "ep")),
        ),
        check_vma=False,
    )
```
